32 devices in a mesh: tmpl: 16 (over z, y, x), sta: 2 (over core).
Axes of the slice: x: 2, y: 2, z: 4, core: 2. Of those that a mesh axis runs over, the one named last changes fastest.
Arguments:
- records: float32 [152, 2048], P('sta', 'tmpl'), may hold values from -6 to 6
- templates: float32 [64, 152, 600], P('tmpl', 'sta'), may hold values from -6 to 6
- offsets: int32 [64, 152], P('tmpl', 'sta'), may hold values from 0 to 425
- available: int32 [64, 152], P('tmpl', 'sta'), may hold values 0 or 1
Outputs:
- detection: float32 [64, 1024], P('tmpl', 'sta')
The draws below stay inside these ranges and needn't reach their ends.
All inputs are finite; a program needn't handle non-finite values. No bound on the sum of `available` on one device may be relied on, other than what follows from the above.
Results may differ from the reference program's by a relative error of at most 0.0066.
Values may be sent and summed in bfloat16 or wider, within the bound.
A program may use at most 64 MiB of HBM per device.

```python
import math
import jax
import jax.numpy as jnp
from jax import lax

CHANNELS = 152
TSAMP = 600
OFFMAX = 425
TEMPLATES = 64
NT = 2048
NLAG = 1024


def draw_records(key, part):
    base_key = jax.random.fold_in(key, 101)
    noise_key, level_key = jax.random.split(base_key, 2)
    offset_level = jax.random.uniform(level_key, (CHANNELS, 1), jnp.float32, -2.0, 2.0)
    drawn_values = offset_level + jax.random.normal(noise_key, (CHANNELS, NT), jnp.float32)
    return jnp.clip(drawn_values, -6.0, 6.0)


def draw_templates(key, part):
    base_key = jax.random.fold_in(key, 202)
    noise_key, level_key = jax.random.split(base_key, 2)
    offset_level = jax.random.uniform(level_key, (TEMPLATES, CHANNELS, 1), jnp.float32, -2.0, 2.0)
    drawn_values = offset_level + jax.random.normal(noise_key, (TEMPLATES, CHANNELS, TSAMP), jnp.float32)
    return jnp.clip(drawn_values, -6.0, 6.0)


def place_ends(array, rng, least, high):
    index_at = [jax.random.randint(jax.random.fold_in(rng, axis), (), 0, length) for axis, length in enumerate(array.shape)]
    widest = array.shape.index(max(array.shape))
    beside = index_at[:widest] + [(index_at[widest] + 1) % array.shape[widest]] + index_at[widest + 1:]
    return array.at[tuple(index_at)].set(least).at[tuple(beside)].set(high)


def setup_inputs(seed: int = 0) -> dict:
    seeds = jax.random.split(jax.random.key(seed), 5)
    records = draw_records(jax.random.fold_in(seeds[4], 71), 0)
    templates = draw_templates(jax.random.fold_in(seeds[4], 71), 0)
    offsets = place_ends(jax.random.randint(seeds[2], (TEMPLATES, CHANNELS), 0, OFFMAX + 1), jax.random.fold_in(seeds[2], 1), 0, OFFMAX).astype(jnp.int32)
    available = place_ends((jax.random.randint(seeds[3], (TEMPLATES, CHANNELS), 0, 4) < 3).astype(jnp.int32), jax.random.fold_in(seeds[3], 1), 0, 1)
    return {"records": records, "templates": templates, "offsets": offsets, "available": available}


def scale_from(running, squared, length, positions):
    first = running[:, length:length + positions] - running[:, :positions]
    second = squared[:, length:length + positions] - squared[:, :positions]
    energy = second - first * first / length
    return 1.0 / jnp.sqrt(energy + 1e-05)

def framed(records_low, count, width, step):
    pieces = width // step
    total = (count + pieces - 1) * step
    padded = jnp.pad(records_low, ((0, 0), (0, total - records_low.shape[1])))
    rows_cut = padded.reshape(records_low.shape[0], count + pieces - 1, step)
    frames = jnp.stack([rows_cut[:, piece:piece + count] for piece in range(pieces)], axis=2)
    return frames.reshape(records_low.shape[0], count, width)

def shifted_copies(centred_low, width, step):
    length = centred_low.shape[2]
    padded = jnp.pad(centred_low, ((0, 0), (0, 0), (0, width + 1 - length)))
    tiled = jnp.tile(padded, (1, 1, step))[:, :, :step * width]
    return tiled.reshape(centred_low.shape[0], centred_low.shape[1], step, width)

def pick_lags(values, starts, count):
    return jax.vmap(jax.vmap(lambda series, start: lax.dynamic_slice_in_dim(series, start, count)))(values, starts)

def reference(records, templates, offsets, available):
    positions = NLAG + OFFMAX
    step = 32
    width = step * ((TSAMP + 2 * step - 2) // step)
    count = (positions + step - 1) // step
    anchor = jnp.zeros((records.shape[0], 1), records.dtype)
    running = jnp.concatenate([anchor, jnp.cumsum(records, axis=1)], axis=1)
    squared = jnp.concatenate([anchor, jnp.cumsum(records * records, axis=1)], axis=1)
    scale = scale_from(running, squared, TSAMP, positions)
    frames = framed(records.astype(jnp.bfloat16), count, width, step).astype(jnp.float32)
    group_size = math.gcd(TEMPLATES, 4)
    groups = TEMPLATES // group_size

    def stack_group(inputs):
        shapes, starts, present = inputs
        centred = shapes - lax.optimization_barrier(jnp.mean(shapes, axis=2, keepdims=True))
        norms = jnp.sqrt(lax.optimization_barrier(jnp.sum(centred * centred, axis=2)) + 1e-05)
        copies = shifted_copies(centred.astype(jnp.bfloat16), width, step).astype(jnp.float32)
        correlated = jnp.einsum('tcsw,cbw->tcbs', copies, frames, precision=lax.Precision.HIGHEST)
        correlated = correlated.reshape(group_size, CHANNELS, count * step)[:, :, :positions]
        picked = pick_lags(correlated * scale[None], starts, NLAG)
        return lax.optimization_barrier(jnp.sum(picked * (present.astype(jnp.float32) / norms)[:, :, None], axis=1))
    stack = lax.map(stack_group, (templates.reshape(groups, group_size, CHANNELS, TSAMP), offsets.reshape(groups, group_size, CHANNELS).astype(jnp.int32), available.reshape(groups, group_size, CHANNELS)))
    stack = stack.reshape(TEMPLATES, NLAG)
    power = lax.optimization_barrier(jnp.mean(stack * stack, axis=1, keepdims=True))
    return stack / jnp.sqrt(power + 1e-05)
```

```python
import functools

import jax
import jax.numpy as jnp
from jax import lax
from jax.experimental import pallas as pl
from jax.experimental.pallas import tpu as pltpu
from jax.sharding import PartitionSpec as P

OFFMAX = 425
LANES = 128
STEP = 32
PARTS = LANES // STEP


def round_up(value, unit):
    return (value + unit - 1) // unit * unit


def largest_divisor(value, most):
    return max(d for d in range(1, most + 1) if value % d == 0)


def split_three(values):
    high = values.astype(jnp.bfloat16)
    rest = values - high.astype(jnp.float32)
    middle = rest.astype(jnp.bfloat16)
    low = (rest - middle.astype(jnp.float32)).astype(jnp.bfloat16)
    return jnp.concatenate([high, middle, low], axis=1)


def correlate_kernel(
    sizes, offsets_ref, available_ref, records_ref, templates_ref, out_ref,
    centred_ref, inverse_ref, rows_ref, sums_ref, scale_ref, shifted_ref, copies_ref, picks_ref,
):
    templ_here, channels, length, blocks, lag_rows, pos_rows, pad_rows, width, group = sizes
    whole, part = length // LANES, length % LANES
    lane = lax.broadcasted_iota(jnp.int32, (1, LANES), 1)

    centred_ref[...] = jnp.zeros_like(centred_ref)
    for t in range(templ_here):
        shapes = templates_ref[t]
        centred = shapes - jnp.sum(shapes, axis=1, keepdims=True) / length
        power = jnp.sum(centred * centred, axis=1, keepdims=True)
        centred_ref[t, :, :length] = centred
        inverse_ref[t] = jnp.broadcast_to(1.0 / jnp.sqrt(power + 1e-05), (channels, LANES))

    row = lax.broadcasted_iota(jnp.int32, (LANES, 2 * LANES), 0)
    column = lax.broadcasted_iota(jnp.int32, (LANES, 2 * LANES), 1)
    ones = jnp.where((row < column) | (column >= LANES), 1.0, 0.0).astype(jnp.bfloat16)
    ones = jnp.concatenate([ones, ones, ones], axis=0)
    rows_ref[...] = jnp.zeros_like(rows_ref)
    sums_ref[...] = jnp.zeros_like(sums_ref)

    def scale_group(g, carry):
        block = records_ref[pl.ds(g * group, group)].reshape(group * blocks, LANES)
        both = jnp.concatenate([split_three(block), split_three(block * block)], axis=0)
        sums = jnp.dot(both, ones, preferred_element_type=jnp.float32)
        for i in range(group):
            windows = []
            for kind in range(2):
                at = (kind * group + i) * blocks
                slot = i * 2 + kind
                sums_ref[slot, :blocks, :] = sums[at : at + blocks]
                inside = lambda first: sums_ref[slot, first : first + pos_rows, :LANES]
                total = lambda first: sums_ref[slot, first : first + pos_rows, LANES:]
                near, far = inside(whole), inside(whole + 1)
                if part:
                    near = pltpu.roll(near, LANES - part, 1)
                    far = pltpu.roll(far, LANES - part, 1)
                window = jnp.where(lane < LANES - part, near, far + total(whole)) - inside(0)
                for b in range(whole):
                    window = window + total(b)
                windows.append(window)
            energy = windows[1] - windows[0] * windows[0] / length
            scale_ref[g * group + i] = 1.0 / jnp.sqrt(energy + 1e-05)
        return carry

    lax.fori_loop(0, channels // group, scale_group, 0)

    def channel(c, slot, totals):
        rows_ref[slot, :blocks, :] = records_ref[c]
        reach = pad_rows - 8
        here = rows_ref[slot, :reach, :]
        after = rows_ref[slot, 1 : reach + 1, :]
        for u in range(PARTS):
            if u == 0:
                moved = here
            else:
                moved = jnp.where(
                    lane < LANES - STEP * u,
                    pltpu.roll(here, LANES - STEP * u, 1),
                    pltpu.roll(after, LANES - STEP * u, 1),
                )
            shifted_ref[slot, u, :reach, :] = moved
        frames = jnp.concatenate(
            [
                jnp.concatenate(
                    [
                        shifted_ref[slot, u, j : j + pos_rows, :].astype(jnp.bfloat16)
                        for j in range(width // LANES)
                    ],
                    axis=1,
                )
                for u in range(PARTS)
            ],
            axis=0,
        )
        for t in range(templ_here):
            wave = jnp.broadcast_to(centred_ref[t, pl.ds(c, 1), :], (8, width))
            first = pltpu.roll(wave, 0, 1, stride=1, stride_axis=0)
            for h in range(STEP // 16):
                pair = [
                    first if s == 0 else pltpu.roll(first, s, 1) for s in (16 * h, 16 * h + 8)
                ]
                copies_ref[slot, pl.ds(t * STEP + 16 * h, 16), :] = jnp.concatenate(
                    pair, axis=0
                ).astype(jnp.bfloat16)
        product = lax.dot_general(
            frames, copies_ref[slot], (((1,), (1,)), ((), ())), preferred_element_type=jnp.float32
        )
        scale = scale_ref[c]
        turned = {}
        for u in range(PARTS):
            piece = product[u * pos_rows : (u + 1) * pos_rows]
            for k in range(PARTS):
                turned[u, k] = piece if k == 0 else pltpu.roll(piece, STEP * k, 1)
        result = []
        for t in range(templ_here):
            values = turned[0, (-t) % PARTS]
            for u in range(1, PARTS):
                values = jnp.where(lane >= STEP * u, turned[u, (u - t) % PARTS], values)
            picks_ref[slot, t] = values * scale
            offset = offsets_ref[t, c]
            down, right = offset // LANES, offset % LANES
            near = picks_ref[slot, t, pl.ds(down, lag_rows), :]
            far = picks_ref[slot, t, pl.ds(down + 1, lag_rows), :]
            picked = jnp.where(lane >= right, near, far)
            weight = inverse_ref[t, pl.ds(c, 1), :] * available_ref[t, c].astype(jnp.float32)
            picked = pltpu.roll(picked * weight, (LANES - right) % LANES, 1)
            result.append(totals[t] + picked)
        return tuple(result)

    def channel_group(g, totals):
        for i in range(group):
            totals = channel(g * group + i, i, totals)
        return totals

    empty = tuple(jnp.zeros((lag_rows, LANES), jnp.float32) for _ in range(templ_here))
    totals = lax.fori_loop(0, channels // group, channel_group, empty)
    for t in range(templ_here):
        out_ref[t] = totals[t]


def correlate(records, templates, offsets, available):
    channels, blocks, _ = records.shape
    templ_here, _, length = templates.shape
    lag_count = blocks * LANES - OFFMAX - length + 1
    lag_rows = lag_count // LANES
    pos_rows = round_up(lag_rows + (OFFMAX + LANES - 1) // LANES, 16)
    width = round_up(length + STEP - 1, LANES)
    pad_rows = round_up(max(pos_rows + width // LANES, blocks) + 1, 8) + 8
    group = largest_divisor(channels, 4)
    sizes = (templ_here, channels, length, blocks, lag_rows, pos_rows, pad_rows, width, group)
    macs = channels * templ_here * STEP * width * PARTS * pos_rows
    return pl.pallas_call(
        functools.partial(correlate_kernel, sizes),
        out_shape=jax.ShapeDtypeStruct((templ_here, lag_rows, LANES), jnp.float32),
        in_specs=[pl.BlockSpec(memory_space=pltpu.SMEM)] * 2
        + [pl.BlockSpec(memory_space=pltpu.VMEM)] * 2,
        out_specs=pl.BlockSpec(memory_space=pltpu.VMEM),
        scratch_shapes=[
            pltpu.VMEM((templ_here, channels, width), jnp.float32),
            pltpu.VMEM((templ_here, channels, LANES), jnp.float32),
            pltpu.VMEM((group, pad_rows, LANES), jnp.float32),
            pltpu.VMEM((2 * group, pad_rows, 2 * LANES), jnp.float32),
            pltpu.VMEM((channels, pos_rows, LANES), jnp.float32),
            pltpu.VMEM((group, PARTS, pad_rows, LANES), jnp.float32),
            pltpu.VMEM((group, templ_here * STEP, width), jnp.bfloat16),
            pltpu.VMEM((group, templ_here, pos_rows, LANES), jnp.float32),
        ],
        compiler_params=pltpu.CompilerParams(vmem_limit_bytes=32 * 1024 * 1024),
        cost_estimate=pl.CostEstimate(
            flops=2 * macs, bytes_accessed=4 * (records.size + templates.size), transcendentals=0
        ),
    )(offsets, available, records, templates)


def shards(records, templates, offsets, available):
    channels_here = records.shape[0]
    whole = lax.all_gather(records, "tmpl", axis=1, tiled=True)
    whole = whole.reshape(channels_here, whole.shape[1] // LANES, LANES)
    partial = correlate(whole, templates, offsets, available)
    partial_stack = partial.reshape(partial.shape[0], -1)
    lag_count = partial_stack.shape[1]
    share = lag_count // lax.axis_size("sta")
    full_stack = lax.psum(partial_stack, "sta")
    power = jnp.mean(full_stack * full_stack, axis=1, keepdims=True)
    mine = lax.dynamic_slice_in_dim(full_stack, lax.axis_index("sta") * share, share, 1)
    return mine / jnp.sqrt(power + 1e-05)


def solution(mesh):
    in_specs = (P("sta", "tmpl"), P("tmpl", "sta", None), P("tmpl", "sta"), P("tmpl", "sta"))
    out_specs = P("tmpl", "sta")
    return jax.shard_map(shards, mesh=mesh, in_specs=in_specs, out_specs=out_specs, check_vma=False)
```

```python
import functools

import jax
import jax.numpy as jnp
from jax import lax
from jax.experimental import pallas as pl
from jax.experimental.pallas import tpu as pltpu
from jax.sharding import PartitionSpec as P

OFFMAX = 425
LANES = 128
STEP = 32
PARTS = LANES // STEP


def round_up(value, unit):
    return (value + unit - 1) // unit * unit


def largest_divisor(value, most):
    return max(d for d in range(1, most + 1) if value % d == 0)


def split_three(values):
    high = values.astype(jnp.bfloat16)
    rest = values - high.astype(jnp.float32)
    middle = rest.astype(jnp.bfloat16)
    low = (rest - middle.astype(jnp.float32)).astype(jnp.bfloat16)
    return jnp.concatenate([high, middle, low], axis=1)


def detect_kernel(
    sizes, offsets_ref, available_ref, records_ref, templates_ref, out_ref,
    gathered_ref, series_ref, centred_ref, inverse_ref, sums_ref, scale_ref, shifted_ref,
    copies_ref, picks_ref, stacks_ref, send_near, recv_near, send_far, recv_far, send_stack, recv_stack,
):
    (templ_here, channels, length, outer, inner, stations, lag_rows, pos_rows, pad_rows, width,
     group, slot_rows) = sizes
    blocks = outer * inner
    whole, part = length // LANES, length % LANES
    lane = lax.broadcasted_iota(jnp.int32, (1, LANES), 1)
    place, station = lax.axis_index("tmpl"), lax.axis_index("sta")
    mine_out, mine_in = place // inner, place % inner

    def far_peer(k):
        return (lax.rem(mine_out + k, outer) * inner + mine_in, station)

    def near_peer(k):
        return (mine_out * inner + lax.rem(mine_in + k, inner), station)

    def stack_peer(k):
        return (place, lax.rem(station + k, stations))

    peers = [far_peer(k) for k in range(1, outer)]
    peers += [near_peer(k) for k in range(1, inner)]
    peers += [stack_peer(k) for k in range(1, stations)]
    barrier = pltpu.get_barrier_semaphore()
    for peer in peers:
        pl.semaphore_signal(barrier, inc=1, device_id=peer, device_id_type=pl.DeviceIdType.MESH)

    own = pl.ds(pl.multiple_of((mine_in * outer + mine_out) * slot_rows, 8), slot_rows)
    if slot_rows > channels:
        tail = jnp.zeros((slot_rows - channels, LANES), jnp.float32)
        gathered_ref[own, :] = jnp.concatenate([records_ref[...], tail], axis=0)
    else:
        gathered_ref[own, :] = records_ref[...]
    pl.semaphore_wait(barrier, len(peers))

    def send(part_ref, send_sem, recv_sem, peer):
        copy = pltpu.make_async_remote_copy(
            src_ref=part_ref, dst_ref=part_ref, send_sem=send_sem, recv_sem=recv_sem,
            device_id=peer, device_id_type=pl.DeviceIdType.MESH,
        )
        copy.start()
        return copy

    far_copies = [
        send(gathered_ref.at[own], send_far.at[k], recv_far.at[k], far_peer(k))
        for k in range(1, outer)
    ]

    centred_ref[...] = jnp.zeros_like(centred_ref)
    for t in range(templ_here):
        shapes = templates_ref[t]
        centred = shapes - jnp.sum(shapes, axis=1, keepdims=True) / length
        power = jnp.sum(centred * centred, axis=1, keepdims=True)
        centred_ref[t, :, :length] = centred
        inverse_ref[t] = jnp.broadcast_to(1.0 / jnp.sqrt(power + 1e-05), (channels, LANES))
    series_ref[...] = jnp.zeros_like(series_ref)
    sums_ref[...] = jnp.zeros_like(sums_ref)

    def delay_group(g, carry):
        for i in range(group):
            c = g * group + i
            for t in range(templ_here):
                wave = jnp.broadcast_to(centred_ref[t, pl.ds(c, 1), :], (8, width))
                first = pltpu.roll(wave, 0, 1, stride=1, stride_axis=0)
                for h in range(STEP // 16):
                    pair = [
                        first if s == 0 else pltpu.roll(first, s, 1)
                        for s in (16 * h, 16 * h + 8)
                    ]
                    copies_ref[c, t * STEP + 16 * h : t * STEP + 16 * h + 16, :] = (
                        jnp.concatenate(pair, axis=0).astype(jnp.bfloat16)
                    )
        return carry

    groups = channels // group
    early = groups // 3
    lax.fori_loop(0, early, delay_group, 0)
    for copy in far_copies:
        copy.wait_recv()
    lane_rows = pl.ds(pl.multiple_of(mine_in * outer * slot_rows, 8), outer * slot_rows)
    near_copies = [
        send(gathered_ref.at[lane_rows], send_near.at[k], recv_near.at[k], near_peer(k))
        for k in range(1, inner)
    ]
    lax.fori_loop(early, groups, delay_group, 0)
    for copy in near_copies:
        copy.wait_recv()
    for copy in far_copies + near_copies:
        copy.wait_send()

    row = lax.broadcasted_iota(jnp.int32, (LANES, 2 * LANES), 0)
    column = lax.broadcasted_iota(jnp.int32, (LANES, 2 * LANES), 1)
    ones = jnp.where((row < column) | (column >= LANES), 1.0, 0.0).astype(jnp.bfloat16)
    ones = jnp.concatenate([ones, ones, ones], axis=0)

    def scale_group(g, carry):
        for i in range(group):
            c = g * group + i
            for o in range(outer):
                series_ref[c, o * inner : (o + 1) * inner, :] = gathered_ref[
                    pl.ds(o * slot_rows + c, inner, stride=outer * slot_rows), :
                ]
        block = jnp.concatenate(
            [series_ref[g * group + i, :blocks, :] for i in range(group)], axis=0
        )
        both = jnp.concatenate([split_three(block), split_three(block * block)], axis=0)
        sums = jnp.dot(both, ones, preferred_element_type=jnp.float32)
        for i in range(group):
            windows = []
            for kind in range(2):
                at = (kind * group + i) * blocks
                slot = i * 2 + kind
                sums_ref[slot, :blocks, :] = sums[at : at + blocks]
                inside = lambda first: sums_ref[slot, first : first + pos_rows, :LANES]
                total = lambda first: sums_ref[slot, first : first + pos_rows, LANES:]
                near, far = inside(whole), inside(whole + 1)
                if part:
                    near = pltpu.roll(near, LANES - part, 1)
                    far = pltpu.roll(far, LANES - part, 1)
                window = jnp.where(lane < LANES - part, near, far + total(whole)) - inside(0)
                for b in range(whole):
                    window = window + total(b)
                windows.append(window)
            energy = windows[1] - windows[0] * windows[0] / length
            scale_ref[g * group + i] = 1.0 / jnp.sqrt(energy + 1e-05)
        return carry

    lax.fori_loop(0, groups, scale_group, 0)

    def channel(c, slot, totals):
        reach = pad_rows - 8
        here = series_ref[c, :reach, :]
        after = series_ref[c, 1 : reach + 1, :]
        for u in range(PARTS):
            if u == 0:
                moved = here
            else:
                moved = jnp.where(
                    lane < LANES - STEP * u,
                    pltpu.roll(here, LANES - STEP * u, 1),
                    pltpu.roll(after, LANES - STEP * u, 1),
                )
            shifted_ref[slot, u, :reach, :] = moved
        frames = jnp.concatenate(
            [
                jnp.concatenate(
                    [
                        shifted_ref[slot, u, j : j + pos_rows, :].astype(jnp.bfloat16)
                        for j in range(width // LANES)
                    ],
                    axis=1,
                )
                for u in range(PARTS)
            ],
            axis=0,
        )
        product = lax.dot_general(
            frames, copies_ref[c], (((1,), (1,)), ((), ())), preferred_element_type=jnp.float32
        )
        scale = scale_ref[c]
        turned = {}
        for u in range(PARTS):
            piece = product[u * pos_rows : (u + 1) * pos_rows]
            for k in range(PARTS):
                turned[u, k] = piece if k == 0 else pltpu.roll(piece, STEP * k, 1)
        result = []
        for t in range(templ_here):
            values = turned[0, (-t) % PARTS]
            for u in range(1, PARTS):
                values = jnp.where(lane >= STEP * u, turned[u, (u - t) % PARTS], values)
            picks_ref[slot, t] = values * scale
            offset = offsets_ref[t, c]
            down, right = offset // LANES, offset % LANES
            wanted = jnp.where(lane < right, down + 1, down)
            picked = picks_ref[slot, t, :lag_rows, :]
            for d in range(1, (OFFMAX + LANES - 1) // LANES + 1):
                picked = jnp.where(wanted == d, picks_ref[slot, t, d : d + lag_rows, :], picked)
            weight = inverse_ref[t, pl.ds(c, 1), :] * available_ref[t, c].astype(jnp.float32)
            picked = pltpu.roll(picked * weight, (LANES - right) % LANES, 1)
            result.append(totals[t] + picked)
        return tuple(result)

    def channel_group(g, totals):
        for i in range(group):
            totals = channel(g * group + i, i, totals)
        return totals

    empty = tuple(jnp.zeros((lag_rows, LANES), jnp.float32) for _ in range(templ_here))
    totals = lax.fori_loop(0, groups, channel_group, empty)

    for t in range(templ_here):
        stacks_ref[station, t] = totals[t]
    stack_copies = [
        send(stacks_ref.at[station], send_stack.at[k], recv_stack.at[k], stack_peer(k))
        for k in range(1, stations)
    ]
    for copy in stack_copies:
        copy.wait_recv()
    share = lag_rows // stations
    for t in range(templ_here):
        full, mine = stacks_ref[0, t], stacks_ref[0, t, pl.ds(station * share, share), :]
        for s in range(1, stations):
            full = full + stacks_ref[s, t]
            mine = mine + stacks_ref[s, t, pl.ds(station * share, share), :]
        power = jnp.sum(jnp.sum(full * full, axis=1, keepdims=True), axis=0, keepdims=True)
        mine = mine / jnp.sqrt(power / (lag_rows * LANES) + 1e-05)
        for r in range(share):
            out_ref[t : t + 1, r * LANES : (r + 1) * LANES] = mine[r : r + 1]
    for copy in stack_copies:
        copy.wait_send()


def shards(records, templates, offsets, available):
    channels, _ = records.shape
    templ_here, _, length = templates.shape
    blocks, stations = lax.axis_size("tmpl"), lax.axis_size("sta")
    inner = largest_divisor(blocks, 4)
    outer = blocks // inner
    lag_rows = (blocks * LANES - OFFMAX - length + 1) // LANES
    reach_rows = (OFFMAX + LANES - 1) // LANES
    pos_rows = round_up(lag_rows + reach_rows, 16)
    width = round_up(length + STEP - 1, LANES)
    pad_rows = round_up(max(pos_rows + width // LANES, blocks) + 1, 8) + 8
    group = largest_divisor(channels, 4)
    slot_rows = round_up(channels, 8)
    sizes = (templ_here, channels, length, outer, inner, stations, lag_rows, pos_rows, pad_rows,
             width, group, slot_rows)
    macs = channels * templ_here * STEP * width * PARTS * pos_rows
    return pl.pallas_call(
        functools.partial(detect_kernel, sizes),
        out_shape=jax.ShapeDtypeStruct((templ_here, lag_rows // stations * LANES), jnp.float32),
        in_specs=[pl.BlockSpec(memory_space=pltpu.SMEM)] * 2
        + [pl.BlockSpec(memory_space=pltpu.VMEM)] * 2,
        out_specs=pl.BlockSpec(memory_space=pltpu.VMEM),
        scratch_shapes=[
            pltpu.VMEM((blocks * slot_rows, LANES), jnp.float32),
            pltpu.VMEM((channels, pad_rows, LANES), jnp.float32),
            pltpu.VMEM((templ_here, channels, width), jnp.float32),
            pltpu.VMEM((templ_here, channels, LANES), jnp.float32),
            pltpu.VMEM((2 * group, pad_rows, 2 * LANES), jnp.float32),
            pltpu.VMEM((channels, pos_rows, LANES), jnp.float32),
            pltpu.VMEM((group, PARTS, pad_rows, LANES), jnp.float32),
            pltpu.VMEM((channels, templ_here * STEP, width), jnp.bfloat16),
            pltpu.VMEM((group, templ_here, pos_rows, LANES), jnp.float32),
            pltpu.VMEM((stations, templ_here, lag_rows, LANES), jnp.float32),
        ]
        + [pltpu.SemaphoreType.DMA((inner,))] * 2
        + [pltpu.SemaphoreType.DMA((outer,))] * 2
        + [pltpu.SemaphoreType.DMA((stations,))] * 2,
        compiler_params=pltpu.CompilerParams(
            collective_id=0, has_side_effects=True, vmem_limit_bytes=40 * 1024 * 1024
        ),
        cost_estimate=pl.CostEstimate(
            flops=2 * macs, bytes_accessed=4 * (records.size + templates.size), transcendentals=0
        ),
    )(offsets, available, records, templates)


def solution(mesh):
    in_specs = (P("sta", "tmpl"), P("tmpl", "sta", None), P("tmpl", "sta"), P("tmpl", "sta"))
    out_specs = P("tmpl", "sta")
    return jax.shard_map(shards, mesh=mesh, in_specs=in_specs, out_specs=out_specs, check_vma=False)
```

```python
import functools

import jax
import jax.numpy as jnp
from jax import lax
from jax.experimental import pallas as pl
from jax.experimental.pallas import tpu as pltpu
from jax.sharding import PartitionSpec as P

OFFMAX = 425
LANES = 128
STEP = 32
PARTS = LANES // STEP


def round_up(value, unit):
    return (value + unit - 1) // unit * unit


def largest_divisor(value, most):
    return max(d for d in range(1, most + 1) if value % d == 0)


def split_three(values):
    high = values.astype(jnp.bfloat16)
    rest = values - high.astype(jnp.float32)
    middle = rest.astype(jnp.bfloat16)
    low = (rest - middle.astype(jnp.float32)).astype(jnp.bfloat16)
    return jnp.concatenate([high, middle, low], axis=1)


def detect_kernel(
    sizes, offsets_ref, available_ref, records_ref, templates_hbm, out_ref,
    templates_ref, gathered_ref, series_ref, centred_ref, inverse_ref, sums_ref, shifted_ref,
    copies_ref, picks_ref, stacks_ref, load_sem, send_near, recv_near, send_far, recv_far,
    send_stack, recv_stack,
):
    (templ_here, channels, length, outer, inner, stations, lag_rows, pos_rows, pad_rows, width,
     group, chunk) = sizes
    blocks = outer * inner
    chunks = round_up(channels, chunk) // chunk
    whole, part = length // LANES, length % LANES
    lane = lax.broadcasted_iota(jnp.int32, (1, LANES), 1)
    place, station = lax.axis_index("tmpl"), lax.axis_index("sta")
    mine_out, mine_in = place // inner, place % inner

    def far_peer(k):
        return (lax.rem(mine_out + k, outer) * inner + mine_in, station)

    def near_peer(k):
        return (mine_out * inner + lax.rem(mine_in + k, inner), station)

    def stack_peer(k):
        return (place, lax.rem(station + k, stations))

    peers = [far_peer(k) for k in range(1, outer)]
    peers += [near_peer(k) for k in range(1, inner)]
    peers += [stack_peer(k) for k in range(1, stations)]
    barrier = pltpu.get_barrier_semaphore()
    for peer in peers:
        pl.semaphore_signal(barrier, inc=1, device_id=peer, device_id_type=pl.DeviceIdType.MESH)

    load = pltpu.make_async_copy(templates_hbm, templates_ref, load_sem.at[0])
    load.start()

    def own_rows(n):
        first = ((n * inner + mine_in) * outer + mine_out) * chunk
        return gathered_ref.at[pl.ds(pl.multiple_of(first, 8), chunk)]

    def line_rows(n):
        first = (n * inner + mine_in) * outer * chunk
        return gathered_ref.at[pl.ds(pl.multiple_of(first, 8), outer * chunk)]

    for n in range(chunks):
        rows = records_ref[n * chunk : min((n + 1) * chunk, channels), :]
        if rows.shape[0] < chunk:
            tail = jnp.zeros((chunk - rows.shape[0], LANES), jnp.float32)
            rows = jnp.concatenate([rows, tail], axis=0)
        own_rows(n)[...] = rows
    pl.semaphore_wait(barrier, len(peers))

    def copy_to(part_ref, send_sem, recv_sem, peer):
        return pltpu.make_async_remote_copy(
            src_ref=part_ref, dst_ref=part_ref, send_sem=send_sem, recv_sem=recv_sem,
            device_id=peer, device_id_type=pl.DeviceIdType.MESH,
        )

    def far_copies(n):
        return [
            copy_to(own_rows(n), send_far.at[k, n], recv_far.at[k, n], far_peer(k))
            for k in range(1, outer)
        ]

    def near_copies(n):
        return [
            copy_to(line_rows(n), send_near.at[k, n], recv_near.at[k, n], near_peer(k))
            for k in range(1, inner)
        ]

    for n in range(chunks):
        for copy in far_copies(n):
            copy.start()

    series_ref[...] = jnp.zeros_like(series_ref)
    sums_ref[...] = jnp.zeros_like(sums_ref)
    centred_ref[...] = jnp.zeros_like(centred_ref)
    load.wait()

    def delay_group(g, carry):
        for i in range(group):
            c = g * group + i
            shapes = templates_ref[c]
            centred = shapes - jnp.sum(shapes, axis=1, keepdims=True) / length
            power = jnp.sum(centred * centred, axis=1, keepdims=True)
            centred_ref[i, :templ_here, :length] = centred
            inverse_ref[c, :templ_here, :] = jnp.broadcast_to(
                1.0 / jnp.sqrt(power + 1e-05), (templ_here, LANES)
            )
            for t in range(templ_here):
                wave = jnp.broadcast_to(centred_ref[i, t : t + 1, :], (8, width))
                first = pltpu.roll(wave, 0, 1, stride=1, stride_axis=0)
                for h in range(STEP // 16):
                    pair = [
                        first if s == 0 else pltpu.roll(first, s, 1)
                        for s in (16 * h, 16 * h + 8)
                    ]
                    copies_ref[c, t * STEP + 16 * h : t * STEP + 16 * h + 16, :] = (
                        jnp.concatenate(pair, axis=0).astype(jnp.bfloat16)
                    )
        return carry

    groups = channels // group
    each = groups // (chunks + 1)

    def forward(n, carry):
        lax.fori_loop(n * each, n * each + each, delay_group, 0)
        for copy in far_copies(n):
            copy.wait_recv()
        for copy in near_copies(n):
            copy.start()
        return carry

    lax.fori_loop(0, chunks, forward, 0)
    lax.fori_loop(chunks * each, groups, delay_group, 0)

    row = lax.broadcasted_iota(jnp.int32, (LANES, 2 * LANES), 0)
    column = lax.broadcasted_iota(jnp.int32, (LANES, 2 * LANES), 1)
    ones = jnp.where((row < column) | (column >= LANES), 1.0, 0.0).astype(jnp.bfloat16)
    ones = jnp.concatenate([ones, ones, ones], axis=0)

    def block_sums(n, count):
        for i in range(count):
            c = n * chunk + i
            for o in range(outer):
                series_ref[c, o * inner : (o + 1) * inner, :] = gathered_ref[
                    pl.ds(n * blocks * chunk + o * chunk + i, inner, stride=outer * chunk), :
                ]
        block = jnp.concatenate(
            [series_ref[n * chunk + i, :blocks, :] for i in range(count)], axis=0
        )
        for kind in range(2):
            parts = split_three(block if kind == 0 else block * block)
            sums = jnp.dot(parts, ones, preferred_element_type=jnp.float32)
            for i in range(count):
                sums_ref[i, kind, :blocks, :] = sums[i * blocks : (i + 1) * blocks]

    def scale_of(i):
        windows = []
        for kind in range(2):
            inside = lambda first: sums_ref[i, kind, first : first + pos_rows, :LANES]
            total = lambda first: sums_ref[i, kind, first : first + pos_rows, LANES:]
            near, far = inside(whole), inside(whole + 1)
            if part:
                near = pltpu.roll(near, LANES - part, 1)
                far = pltpu.roll(far, LANES - part, 1)
            window = jnp.where(lane < LANES - part, near, far + total(whole)) - inside(0)
            for b in range(whole):
                window = window + total(b)
            windows.append(window)
        energy = windows[1] - windows[0] * windows[0] / length
        return 1.0 / jnp.sqrt(energy + 1e-05)

    def channel(c, inside_chunk, slot, totals):
        reach = pad_rows - 8
        for u in range(1, PARTS):
            shifted_ref[slot, u, :reach, :] = pltpu.roll(
                series_ref[c, :reach, :], LANES - STEP * u, 1
            )

        def frame(u, j):
            if u == 0:
                return series_ref[c, j : j + pos_rows, :].astype(jnp.bfloat16)
            return jnp.where(
                lane < LANES - STEP * u,
                shifted_ref[slot, u, j : j + pos_rows, :],
                shifted_ref[slot, u, j + 1 : j + 1 + pos_rows, :],
            ).astype(jnp.bfloat16)

        frames = jnp.concatenate(
            [
                jnp.concatenate(
                    [frame(u, j) for j in range(width // LANES)],
                    axis=1,
                )
                for u in range(PARTS)
            ],
            axis=0,
        )
        product = lax.dot_general(
            frames, copies_ref[c], (((1,), (1,)), ((), ())), preferred_element_type=jnp.float32
        )
        scale = scale_of(inside_chunk)
        turned = {}
        for u in range(PARTS):
            piece = product[u * pos_rows : (u + 1) * pos_rows]
            for k in range(PARTS):
                turned[u, k] = piece if k == 0 else pltpu.roll(piece, STEP * k, 1)
        result = []
        for t in range(templ_here):
            values = turned[0, (-t) % PARTS]
            for u in range(1, PARTS):
                values = jnp.where(lane >= STEP * u, turned[u, (u - t) % PARTS], values)
            picks_ref[slot, t] = values * scale
            offset = offsets_ref[t, c]
            down, right = offset // LANES, offset % LANES
            wanted = jnp.where(lane < right, down + 1, down)
            picked = picks_ref[slot, t, :lag_rows, :]
            for d in range(1, (OFFMAX + LANES - 1) // LANES + 1):
                picked = jnp.where(wanted == d, picks_ref[slot, t, d : d + lag_rows, :], picked)
            weight = inverse_ref[c, t : t + 1, :] * available_ref[t, c].astype(jnp.float32)
            picked = pltpu.roll(picked * weight, (LANES - right) % LANES, 1)
            result.append(totals[t] + picked)
        return tuple(result)

    def one_chunk(n, count, totals):
        for copy in near_copies(n):
            copy.wait_recv()
        block_sums(n, count)

        def channel_group(g, totals):
            for i in range(group):
                totals = channel(n * chunk + g * group + i, g * group + i, i, totals)
            return totals

        return lax.fori_loop(0, count // group, channel_group, totals)

    totals = tuple(jnp.zeros((lag_rows, LANES), jnp.float32) for _ in range(templ_here))
    full_chunks = channels // chunk
    totals = lax.fori_loop(0, full_chunks, lambda n, totals: one_chunk(n, chunk, totals), totals)
    if full_chunks < chunks:
        totals = one_chunk(full_chunks, channels - full_chunks * chunk, totals)

    for t in range(templ_here):
        stacks_ref[station, t] = totals[t]
    stack_copies = [
        copy_to(stacks_ref.at[station], send_stack.at[k], recv_stack.at[k], stack_peer(k))
        for k in range(1, stations)
    ]
    for copy in stack_copies:
        copy.start()
    for copy in stack_copies:
        copy.wait_recv()
    share = lag_rows // stations
    for t in range(templ_here):
        full, mine = stacks_ref[0, t], stacks_ref[0, t, pl.ds(station * share, share), :]
        for s in range(1, stations):
            full = full + stacks_ref[s, t]
            mine = mine + stacks_ref[s, t, pl.ds(station * share, share), :]
        power = jnp.sum(jnp.sum(full * full, axis=1, keepdims=True), axis=0, keepdims=True)
        mine = mine / jnp.sqrt(power / (lag_rows * LANES) + 1e-05)
        for r in range(share):
            out_ref[t : t + 1, r * LANES : (r + 1) * LANES] = mine[r : r + 1]
    for copy in stack_copies:
        copy.wait_send()
    for n in range(chunks):
        for copy in far_copies(n) + near_copies(n):
            copy.wait_send()


def shards(records, templates, offsets, available):
    channels, _ = records.shape
    templ_here, _, length = templates.shape
    blocks, stations = lax.axis_size("tmpl"), lax.axis_size("sta")
    inner = largest_divisor(blocks, 4)
    outer = blocks // inner
    lag_rows = (blocks * LANES - OFFMAX - length + 1) // LANES
    reach_rows = (OFFMAX + LANES - 1) // LANES
    pos_rows = round_up(lag_rows + reach_rows, 16)
    width = round_up(length + STEP - 1, LANES)
    pad_rows = round_up(max(pos_rows + width // LANES, blocks) + 1, 8) + 8
    group = largest_divisor(channels, 4)
    slot_rows = round_up(channels, 8)
    chunk = 16 if slot_rows % 16 == 0 else 8
    chunks = slot_rows // chunk
    sizes = (templ_here, channels, length, outer, inner, stations, lag_rows, pos_rows, pad_rows,
             width, group, chunk)
    macs = channels * templ_here * STEP * width * PARTS * pos_rows
    return pl.pallas_call(
        functools.partial(detect_kernel, sizes),
        out_shape=jax.ShapeDtypeStruct((templ_here, lag_rows // stations * LANES), jnp.float32),
        in_specs=[pl.BlockSpec(memory_space=pltpu.SMEM)] * 2
        + [pl.BlockSpec(memory_space=pltpu.VMEM), pl.BlockSpec(memory_space=pltpu.HBM)],
        out_specs=pl.BlockSpec(memory_space=pltpu.VMEM),
        scratch_shapes=[
            pltpu.VMEM((channels, templ_here, length), jnp.float32),
            pltpu.VMEM((blocks * slot_rows, LANES), jnp.float32),
            pltpu.VMEM((channels, pad_rows, LANES), jnp.float32),
            pltpu.VMEM((group, round_up(templ_here, 8), width), jnp.float32),
            pltpu.VMEM((channels, round_up(templ_here, 8), LANES), jnp.float32),
            pltpu.VMEM((chunk, 2, pad_rows, 2 * LANES), jnp.float32),
            pltpu.VMEM((group, PARTS, pad_rows, LANES), jnp.float32),
            pltpu.VMEM((channels, templ_here * STEP, width), jnp.bfloat16),
            pltpu.VMEM((group, templ_here, pos_rows, LANES), jnp.float32),
            pltpu.VMEM((stations, templ_here, lag_rows, LANES), jnp.float32),
        ]
        + [pltpu.SemaphoreType.DMA((1,))]
        + [pltpu.SemaphoreType.DMA((inner, chunks))] * 2
        + [pltpu.SemaphoreType.DMA((outer, chunks))] * 2
        + [pltpu.SemaphoreType.DMA((stations,))] * 2,
        compiler_params=pltpu.CompilerParams(
            collective_id=0, has_side_effects=True, vmem_limit_bytes=40 * 1024 * 1024
        ),
        cost_estimate=pl.CostEstimate(
            flops=2 * macs, bytes_accessed=4 * (records.size + templates.size), transcendentals=0
        ),
    )(offsets, available, records, jnp.transpose(templates, (1, 0, 2)))


def solution(mesh):
    in_specs = (P("sta", "tmpl"), P("tmpl", "sta", None), P("tmpl", "sta"), P("tmpl", "sta"))
    out_specs = P("tmpl", "sta")
    return jax.shard_map(shards, mesh=mesh, in_specs=in_specs, out_specs=out_specs, check_vma=False)
```

```python
import functools

import jax
import jax.numpy as jnp
from jax import lax
from jax.experimental import pallas as pl
from jax.experimental.pallas import tpu as pltpu
from jax.sharding import PartitionSpec as P

OFFMAX = 425
LANES = 128
STEP = 32
PARTS = LANES // STEP


def round_up(value, unit):
    return (value + unit - 1) // unit * unit


def largest_divisor(value, most):
    return max(d for d in range(1, most + 1) if value % d == 0)


def split_three(values):
    high = values.astype(jnp.bfloat16)
    rest = values - high.astype(jnp.float32)
    middle = rest.astype(jnp.bfloat16)
    low = (rest - middle.astype(jnp.float32)).astype(jnp.bfloat16)
    return jnp.concatenate([high, middle, low], axis=1)


def detect_kernel(
    sizes, offsets_hbm, available_hbm, records_hbm, templates_hbm, out_ref,
    offsets_ref, available_ref, records_ref, templates_ref, gathered_ref, series_ref, centred_ref,
    inverse_ref, sums_ref, scale_ref, shifted_ref, frames_ref, copies_ref, products_ref, picks_ref,
    stacks_ref, load_sem, send_near, recv_near, send_far, recv_far,
    send_stack, recv_stack,
):
    (templ_here, channels, length, outer, inner, stations, lag_rows, pos_rows, pad_rows, width,
     group, chunk) = sizes
    blocks = outer * inner
    chunks = round_up(channels, chunk) // chunk
    whole, part = length // LANES, length % LANES
    lane = lax.broadcasted_iota(jnp.int32, (1, LANES), 1)
    place, station = lax.axis_index("tmpl"), lax.axis_index("sta")
    mine_out, mine_in = place // inner, place % inner

    def far_peer(k):
        return (lax.rem(mine_out + k, outer) * inner + mine_in, station)

    def near_peer(k):
        return (mine_out * inner + lax.rem(mine_in + k, inner), station)

    def stack_peer(k):
        return (place, lax.rem(station + k, stations))

    peers = [far_peer(k) for k in range(1, outer)]
    peers += [near_peer(k) for k in range(1, inner)]
    peers += [stack_peer(k) for k in range(1, stations)]
    barrier = pltpu.get_barrier_semaphore()
    for peer in peers:
        pl.semaphore_signal(barrier, inc=1, device_id=peer, device_id_type=pl.DeviceIdType.MESH)

    loads = [
        pltpu.make_async_copy(source, target, load_sem.at[at])
        for at, (source, target) in enumerate((
            (records_hbm, records_ref), (templates_hbm, templates_ref),
            (offsets_hbm, offsets_ref), (available_hbm, available_ref),
        ))
    ]
    for load in loads:
        load.start()

    def own_rows(n):
        first = ((n * inner + mine_in) * outer + mine_out) * chunk
        return gathered_ref.at[pl.ds(pl.multiple_of(first, 8), chunk)]

    def line_rows(n):
        first = (n * inner + mine_in) * outer * chunk
        return gathered_ref.at[pl.ds(pl.multiple_of(first, 8), outer * chunk)]

    loads[0].wait()
    for n in range(chunks):
        rows = records_ref[n * chunk : min((n + 1) * chunk, channels), :]
        if rows.shape[0] < chunk:
            tail = jnp.zeros((chunk - rows.shape[0], LANES), jnp.float32)
            rows = jnp.concatenate([rows, tail], axis=0)
        own_rows(n)[...] = rows
    pl.semaphore_wait(barrier, len(peers))

    def copy_to(part_ref, send_sem, recv_sem, peer):
        return pltpu.make_async_remote_copy(
            src_ref=part_ref, dst_ref=part_ref, send_sem=send_sem, recv_sem=recv_sem,
            device_id=peer, device_id_type=pl.DeviceIdType.MESH,
        )

    def far_copies(n):
        return [
            copy_to(own_rows(n), send_far.at[k, n], recv_far.at[k, n], far_peer(k))
            for k in range(1, outer)
        ]

    def near_copies(n):
        return [
            copy_to(line_rows(n), send_near.at[k, n], recv_near.at[k, n], near_peer(k))
            for k in range(1, inner)
        ]

    for n in range(chunks):
        for copy in far_copies(n):
            copy.start()

    for ref in (series_ref, sums_ref, centred_ref, scale_ref, frames_ref, products_ref):
        ref[...] = jnp.zeros_like(ref)
    for load in loads[1:]:
        load.wait()

    def centre_group(g, carry):
        for i in range(group):
            c = g * group + i
            shapes = templates_ref[c]
            centred = shapes - jnp.sum(shapes, axis=1, keepdims=True) / length
            power = jnp.sum(centred * centred, axis=1, keepdims=True)
            centred_ref[c, :templ_here, :length] = centred
            inverse_ref[c, :templ_here, :] = jnp.broadcast_to(
                1.0 / jnp.sqrt(power + 1e-05), (templ_here, LANES)
            )
        return carry

    def delay_group(g, carry):
        for i in range(group):
            c = g * group + i
            for t in range(templ_here):
                wave = jnp.broadcast_to(centred_ref[c, t : t + 1, :], (8, width))
                first = pltpu.roll(wave, 0, 1, stride=1, stride_axis=0)
                for h in range(STEP // 16):
                    pair = [
                        first if s == 0 else pltpu.roll(first, s, 1)
                        for s in (16 * h, 16 * h + 8)
                    ]
                    copies_ref[c, t * STEP + 16 * h : t * STEP + 16 * h + 16, :] = (
                        jnp.concatenate(pair, axis=0).astype(jnp.bfloat16)
                    )
        return carry

    groups = channels // group
    each = groups // (chunks + 1)
    lax.fori_loop(0, groups, centre_group, 0)

    def forward(n, carry):
        lax.fori_loop(n * each, n * each + each, delay_group, 0)
        for copy in far_copies(n):
            copy.wait_recv()
        for copy in near_copies(n):
            copy.start()
        return carry

    lax.fori_loop(0, chunks, forward, 0)
    lax.fori_loop(chunks * each, groups, delay_group, 0)

    row = lax.broadcasted_iota(jnp.int32, (LANES, 2 * LANES), 0)
    column = lax.broadcasted_iota(jnp.int32, (LANES, 2 * LANES), 1)
    ones = jnp.where((row < column) | (column >= LANES), 1.0, 0.0).astype(jnp.bfloat16)
    ones = jnp.concatenate([ones, ones, ones], axis=0)

    def block_sums(n, count):
        for i in range(count):
            c = n * chunk + i
            for o in range(outer):
                series_ref[c, o * inner : (o + 1) * inner, :] = gathered_ref[
                    pl.ds(n * blocks * chunk + o * chunk + i, inner, stride=outer * chunk), :
                ]
        block = jnp.concatenate(
            [series_ref[n * chunk + i, :blocks, :] for i in range(count)], axis=0
        )
        for kind in range(2):
            parts = split_three(block if kind == 0 else block * block)
            sums = jnp.dot(parts, ones, preferred_element_type=jnp.float32)
            for i in range(count):
                sums_ref[i, kind, :blocks, :] = sums[i * blocks : (i + 1) * blocks]

    def scale_of(i):
        windows = []
        for kind in range(2):
            inside = lambda first: sums_ref[i, kind, first : first + pos_rows, :LANES]
            total = lambda first: sums_ref[i, kind, first : first + pos_rows, LANES:]
            near, far = inside(whole), inside(whole + 1)
            if part:
                near = pltpu.roll(near, LANES - part, 1)
                far = pltpu.roll(far, LANES - part, 1)
            window = jnp.where(lane < LANES - part, near, far + total(whole)) - inside(0)
            for b in range(whole):
                window = window + total(b)
            windows.append(window)
        energy = windows[1] - windows[0] * windows[0] / length
        return 1.0 / jnp.sqrt(energy + 1e-05)

    def frame_channel(c, inside_chunk, slot):
        reach = pad_rows - 8
        for u in range(1, PARTS):
            shifted_ref[slot, u, :reach, :] = pltpu.roll(
                series_ref[c, :reach, :], LANES - STEP * u, 1
            )
        for u in range(PARTS):
            for j in range(width // LANES):
                if u == 0:
                    frame = series_ref[c, j : j + pos_rows, :]
                else:
                    frame = jnp.where(
                        lane < LANES - STEP * u,
                        shifted_ref[slot, u, j : j + pos_rows, :],
                        shifted_ref[slot, u, j + 1 : j + 1 + pos_rows, :],
                    )
                frames_ref[
                    slot, u * pos_rows : (u + 1) * pos_rows, j * LANES : (j + 1) * LANES
                ] = frame.astype(jnp.bfloat16)
        scale_ref[c] = scale_of(inside_chunk)

    def multiply_channel(c, slot):
        products_ref[slot] = lax.dot_general(
            frames_ref[slot], copies_ref[c], (((1,), (1,)), ((), ())),
            preferred_element_type=jnp.float32,
        )

    def pick_channel(c, slot, totals):
        scale = scale_ref[c]
        turned = {}
        for u in range(PARTS):
            piece = products_ref[slot, u * pos_rows : (u + 1) * pos_rows, :]
            for k in range(PARTS):
                turned[u, k] = piece if k == 0 else pltpu.roll(piece, STEP * k, 1)
        result = []
        for t in range(templ_here):
            values = turned[0, (-t) % PARTS]
            for u in range(1, PARTS):
                values = jnp.where(lane >= STEP * u, turned[u, (u - t) % PARTS], values)
            picks_ref[slot, t] = values * scale
        for t in range(templ_here):
            offset = offsets_ref[t, c]
            down, right = offset // LANES, offset % LANES
            wanted = jnp.where(lane < right, down + 1, down)
            picked = picks_ref[slot, t, :lag_rows, :]
            for d in range(1, (OFFMAX + LANES - 1) // LANES + 1):
                picked = jnp.where(wanted == d, picks_ref[slot, t, d : d + lag_rows, :], picked)
            weight = inverse_ref[c, t : t + 1, :] * available_ref[t, c].astype(jnp.float32)
            picked = pltpu.roll(picked * weight, (LANES - right) % LANES, 1)
            result.append(totals[t] + picked)
        return tuple(result)

    def pick_group(g, totals):
        for i in range(group):
            totals = pick_channel(g * group + i, i, totals)
        return totals

    def multiply_group(g):
        for i in range(group):
            multiply_channel(g * group + i, i)

    def one_chunk(n, count, totals):
        for copy in near_copies(n):
            copy.wait_recv()
        block_sums(n, count)

        def channel_group(h, totals):
            g = n * (chunk // group) + h
            totals = pick_group((g + groups - 2) % groups, totals)
            multiply_group((g + groups - 1) % groups)
            for i in range(group):
                frame_channel(g * group + i, h * group + i, i)
            return totals

        return lax.fori_loop(0, count // group, channel_group, totals)

    totals = tuple(jnp.zeros((lag_rows, LANES), jnp.float32) for _ in range(templ_here))
    full_chunks = channels // chunk
    totals = lax.fori_loop(0, full_chunks, lambda n, totals: one_chunk(n, chunk, totals), totals)
    if full_chunks < chunks:
        totals = one_chunk(full_chunks, channels - full_chunks * chunk, totals)
    totals = pick_group(groups - 2, totals)
    multiply_group(groups - 1)
    totals = pick_group(groups - 1, totals)

    for t in range(templ_here):
        stacks_ref[station, t] = totals[t]
    stack_copies = [
        copy_to(stacks_ref.at[station], send_stack.at[k], recv_stack.at[k], stack_peer(k))
        for k in range(1, stations)
    ]
    for copy in stack_copies:
        copy.start()
    for copy in stack_copies:
        copy.wait_recv()
    share = lag_rows // stations
    for t in range(templ_here):
        full, mine = stacks_ref[0, t], stacks_ref[0, t, pl.ds(station * share, share), :]
        for s in range(1, stations):
            full = full + stacks_ref[s, t]
            mine = mine + stacks_ref[s, t, pl.ds(station * share, share), :]
        power = jnp.sum(jnp.sum(full * full, axis=1, keepdims=True), axis=0, keepdims=True)
        mine = mine / jnp.sqrt(power / (lag_rows * LANES) + 1e-05)
        for r in range(share):
            out_ref[t : t + 1, r * LANES : (r + 1) * LANES] = mine[r : r + 1]
    for copy in stack_copies:
        copy.wait_send()
    for n in range(chunks):
        for copy in far_copies(n) + near_copies(n):
            copy.wait_send()


def shards(records, templates, offsets, available):
    channels, _ = records.shape
    templ_here, _, length = templates.shape
    blocks, stations = lax.axis_size("tmpl"), lax.axis_size("sta")
    inner = largest_divisor(blocks, 4)
    outer = blocks // inner
    lag_rows = (blocks * LANES - OFFMAX - length + 1) // LANES
    reach_rows = (OFFMAX + LANES - 1) // LANES
    pos_rows = round_up(lag_rows + reach_rows, 16)
    width = round_up(length + STEP - 1, LANES)
    pad_rows = round_up(max(pos_rows + width // LANES, blocks) + 1, 8) + 8
    group = largest_divisor(channels, 4)
    slot_rows = round_up(channels, 8)
    chunk = 16 if slot_rows % 16 == 0 else 8
    chunks = slot_rows // chunk
    sizes = (templ_here, channels, length, outer, inner, stations, lag_rows, pos_rows, pad_rows,
             width, group, chunk)
    macs = channels * templ_here * STEP * width * PARTS * pos_rows
    return pl.pallas_call(
        functools.partial(detect_kernel, sizes),
        out_shape=jax.ShapeDtypeStruct((templ_here, lag_rows // stations * LANES), jnp.float32),
        in_specs=[pl.BlockSpec(memory_space=pltpu.HBM)] * 4,
        out_specs=pl.BlockSpec(memory_space=pltpu.VMEM),
        scratch_shapes=[
            pltpu.SMEM(offsets.shape, jnp.int32),
            pltpu.SMEM(available.shape, jnp.int32),
            pltpu.VMEM((channels, LANES), jnp.float32),
            pltpu.VMEM((channels, templ_here, length), jnp.float32),
            pltpu.VMEM((blocks * slot_rows, LANES), jnp.float32),
            pltpu.VMEM((channels, pad_rows, LANES), jnp.float32),
            pltpu.VMEM((channels, round_up(templ_here, 8), width), jnp.float32),
            pltpu.VMEM((channels, round_up(templ_here, 8), LANES), jnp.float32),
            pltpu.VMEM((chunk, 2, pad_rows, 2 * LANES), jnp.float32),
            pltpu.VMEM((channels, pos_rows, LANES), jnp.float32),
            pltpu.VMEM((group, PARTS, pad_rows, LANES), jnp.float32),
            pltpu.VMEM((group, PARTS * pos_rows, width), jnp.bfloat16),
            pltpu.VMEM((channels, templ_here * STEP, width), jnp.bfloat16),
            pltpu.VMEM((group, PARTS * pos_rows, templ_here * STEP), jnp.float32),
            pltpu.VMEM((group, templ_here, pos_rows, LANES), jnp.float32),
            pltpu.VMEM((stations, templ_here, lag_rows, LANES), jnp.float32),
        ]
        + [pltpu.SemaphoreType.DMA((4,))]
        + [pltpu.SemaphoreType.DMA((inner, chunks))] * 2
        + [pltpu.SemaphoreType.DMA((outer, chunks))] * 2
        + [pltpu.SemaphoreType.DMA((stations,))] * 2,
        compiler_params=pltpu.CompilerParams(
            collective_id=0, has_side_effects=True, vmem_limit_bytes=60 * 1024 * 1024
        ),
        cost_estimate=pl.CostEstimate(
            flops=2 * macs, bytes_accessed=4 * (records.size + templates.size), transcendentals=0
        ),
    )(offsets, available, records, jnp.transpose(templates, (1, 0, 2)))


def solution(mesh):
    in_specs = (P("sta", "tmpl"), P("tmpl", "sta", None), P("tmpl", "sta"), P("tmpl", "sta"))
    out_specs = P("tmpl", "sta")
    return jax.shard_map(shards, mesh=mesh, in_specs=in_specs, out_specs=out_specs, check_vma=False)
```

```python
import functools

import jax
import jax.numpy as jnp
from jax import lax
from jax.experimental import pallas as pl
from jax.experimental.pallas import tpu as pltpu
from jax.sharding import PartitionSpec as P

OFFMAX = 425
LANES = 128
STEP = 32
PARTS = LANES // STEP
CHUNK = 8


def round_up(value, unit):
    return (value + unit - 1) // unit * unit


def largest_divisor(value, most):
    return max(d for d in range(1, most + 1) if value % d == 0)


def split_three(values):
    high = values.astype(jnp.bfloat16)
    rest = values - high.astype(jnp.float32)
    middle = rest.astype(jnp.bfloat16)
    low = (rest - middle.astype(jnp.float32)).astype(jnp.bfloat16)
    return jnp.concatenate([high, middle, low], axis=1)


def detect_kernel(
    sizes, offsets_hbm, available_hbm, records_hbm, templates_hbm, out_ref,
    offsets_ref, available_ref, records_ref, templates_ref, gathered_ref, centred_ref, inverse_ref,
    scale_ref, moved_ref, copies_ref, picks_ref, stacks_ref, load_sem, send_near, recv_near, send_far, recv_far,
    send_stack, recv_stack,
):
    (templ_here, channels, length, outer, inner, stations, lag_rows, need_rows, pos_rows, rows,
     width) = sizes
    blocks = outer * inner
    chunk = CHUNK
    chunks = round_up(channels, chunk) // chunk
    whole, part = length // LANES, length % LANES
    lane = lax.broadcasted_iota(jnp.int32, (1, LANES), 1)
    place, station = lax.axis_index("tmpl"), lax.axis_index("sta")
    mine_out, mine_in = place // inner, place % inner

    def far_peer(k):
        return (lax.rem(mine_out + k, outer) * inner + mine_in, station)

    def near_peer(k):
        return (mine_out * inner + lax.rem(mine_in + k, inner), station)

    def stack_peer(k):
        return (place, lax.rem(station + k, stations))

    peers = [far_peer(k) for k in range(1, outer)]
    peers += [near_peer(k) for k in range(1, inner)]
    peers += [stack_peer(k) for k in range(1, stations)]
    barrier = pltpu.get_barrier_semaphore()
    for peer in peers:
        pl.semaphore_signal(barrier, inc=1, device_id=peer, device_id_type=pl.DeviceIdType.MESH)

    loads = [
        pltpu.make_async_copy(source, target, load_sem.at[at])
        for at, (source, target) in enumerate((
            (records_hbm, records_ref), (templates_hbm, templates_ref),
            (offsets_hbm, offsets_ref), (available_hbm, available_ref),
        ))
    ]
    for load in loads:
        load.start()

    def own_rows(n):
        first = ((n * inner + mine_in) * outer + mine_out) * chunk
        return gathered_ref.at[pl.ds(pl.multiple_of(first, 8), chunk)]

    def line_rows(n):
        first = (n * inner + mine_in) * outer * chunk
        return gathered_ref.at[pl.ds(pl.multiple_of(first, 8), outer * chunk)]

    loads[0].wait()
    for n in range(chunks):
        part_of = records_ref[n * chunk : min((n + 1) * chunk, channels), :]
        if part_of.shape[0] < chunk:
            tail = jnp.zeros((chunk - part_of.shape[0], LANES), jnp.float32)
            part_of = jnp.concatenate([part_of, tail], axis=0)
        own_rows(n)[...] = part_of
    pl.semaphore_wait(barrier, len(peers))

    def copy_to(part_ref, send_sem, recv_sem, peer):
        return pltpu.make_async_remote_copy(
            src_ref=part_ref, dst_ref=part_ref, send_sem=send_sem, recv_sem=recv_sem,
            device_id=peer, device_id_type=pl.DeviceIdType.MESH,
        )

    def far_copies(n):
        return [
            copy_to(own_rows(n), send_far.at[k, n], recv_far.at[k, n], far_peer(k))
            for k in range(1, outer)
        ]

    def near_copies(n):
        return [
            copy_to(line_rows(n), send_near.at[k, n], recv_near.at[k, n], near_peer(k))
            for k in range(1, inner)
        ]

    for n in range(chunks):
        for copy in far_copies(n):
            copy.start()

    for ref in (scale_ref, moved_ref):
        ref[...] = jnp.zeros_like(ref)
    filled = length // LANES * LANES
    centred_ref[:, :, filled:] = jnp.zeros(
        (channels, centred_ref.shape[1], width - filled), jnp.float32
    )
    for load in loads[1:]:
        load.wait()

    def centre_group(g, carry):
        for i in range(group):
            c = g * group + i
            shapes = templates_ref[c]
            centred = shapes - jnp.sum(shapes, axis=1, keepdims=True) / length
            power = jnp.sum(centred * centred, axis=1, keepdims=True)
            centred_ref[c, :templ_here, :length] = centred
            inverse_ref[c, :templ_here, :] = jnp.broadcast_to(
                1.0 / jnp.sqrt(power + 1e-05), (templ_here, LANES)
            )
        return carry

    def delay_channel(c):
        for t in range(templ_here):
            wave = jnp.broadcast_to(centred_ref[c, t : t + 1, :], (8, width))
            first = pltpu.roll(wave, 0, 1, stride=1, stride_axis=0)
            for h in range(STEP // 16):
                pair = [
                    first if s == 0 else pltpu.roll(first, s, 1) for s in (16 * h, 16 * h + 8)
                ]
                copies_ref[c, t * STEP + 16 * h : t * STEP + 16 * h + 16, :] = (
                    jnp.concatenate(pair, axis=0).astype(jnp.bfloat16)
                )

    group = largest_divisor(channels, 4)
    lax.fori_loop(0, channels // group, centre_group, 0)
    full_chunks = channels // chunk
    ahead = max(1, chunks // 2)
    each = chunks // ahead

    def forward(n):
        for copy in far_copies(n):
            copy.wait_recv()
        for copy in near_copies(n):
            copy.start()

    def early(n, carry):
        for i in range(chunk):
            delay_channel(n * chunk + i)
        for k in range(each):
            forward(n * each + k)
        return carry

    lax.fori_loop(0, ahead, early, 0)
    for n in range(ahead * each, chunks):
        forward(n)
    for c in range(full_chunks * chunk, channels):
        delay_channel(c)

    row = lax.broadcasted_iota(jnp.int32, (LANES, 2 * LANES), 0)
    column = lax.broadcasted_iota(jnp.int32, (LANES, 2 * LANES), 1)
    ones = jnp.where((row < column) | (column >= LANES), 1.0, 0.0).astype(jnp.bfloat16)
    ones = jnp.concatenate([ones, ones, ones], axis=0)

    def prepare(n):
        series = []
        for a in range(blocks):
            first = ((n * inner + a % inner) * outer + a // inner) * chunk
            series.append(gathered_ref[pl.ds(pl.multiple_of(first, 8), chunk), :])
        nothing = jnp.zeros((chunk, LANES), jnp.float32)
        at = lambda values, a: values[a] if a < blocks else nothing
        for u in range(PARTS):
            if u == 0:
                moved = series
            else:
                turned = [pltpu.roll(values, LANES - STEP * u, 1) for values in series]
                moved = [
                    jnp.where(lane < LANES - STEP * u, turned[a], at(turned, a + 1))
                    for a in range(blocks)
                ]
            for a in range(blocks):
                moved_ref[(u * rows + a) * chunk : (u * rows + a + 1) * chunk, :] = moved[a]
        block = jnp.concatenate(series, axis=0)
        both = jnp.concatenate([split_three(block), split_three(block * block)], axis=0)
        sums = jnp.dot(both, ones, preferred_element_type=jnp.float32)
        windows = []
        for kind in range(2):
            piece = [
                sums[(kind * blocks + a) * chunk : (kind * blocks + a + 1) * chunk]
                for a in range(blocks)
            ]
            inside = [values[:, :LANES] for values in piece]
            total = [values[:, LANES:] for values in piece]
            turned = [pltpu.roll(values, (LANES - part) % LANES, 1) for values in inside]
            window = []
            for a in range(need_rows):
                end = jnp.where(
                    lane < LANES - part,
                    at(turned, a + whole),
                    at(turned, a + whole + 1) + at(total, a + whole),
                )
                end = end - at(inside, a)
                for b in range(whole):
                    end = end + at(total, a + b)
                window.append(end)
            windows.append(window)
        for a in range(need_rows):
            energy = windows[1][a] - windows[0][a] * windows[0][a] / length
            scale_ref[a * chunk : (a + 1) * chunk, :] = lax.rsqrt(energy + 1e-05)

    def channel(n, i, totals):
        c = n * chunk + i
        frames = jnp.concatenate(
            [
                jnp.concatenate(
                    [
                        moved_ref[pl.ds((u * rows + j) * chunk + i, pos_rows, stride=chunk), :]
                        .astype(jnp.bfloat16)
                        for j in range(width // LANES)
                    ],
                    axis=1,
                )
                for u in range(PARTS)
            ],
            axis=0,
        )
        product = lax.dot_general(
            frames, copies_ref[c], (((1,), (1,)), ((), ())), preferred_element_type=jnp.float32
        )
        scale = scale_ref[pl.ds(i, pos_rows, stride=chunk), :]
        turned = {}
        for u in range(PARTS):
            piece = product[u * pos_rows : (u + 1) * pos_rows]
            for k in range(PARTS):
                turned[u, k] = piece if k == 0 else pltpu.roll(piece, STEP * k, 1)
        result = []
        for t in range(templ_here):
            values = turned[0, (-t) % PARTS]
            for u in range(1, PARTS):
                values = jnp.where(lane >= STEP * u, turned[u, (u - t) % PARTS], values)
            picks_ref[i, t] = values * scale
            offset = offsets_ref[t, c]
            down, right = offset // LANES, offset % LANES
            wanted = jnp.where(lane < right, down + 1, down)
            picked = picks_ref[i, t, :lag_rows, :]
            for d in range(1, (OFFMAX + LANES - 1) // LANES + 1):
                picked = jnp.where(wanted == d, picks_ref[i, t, d : d + lag_rows, :], picked)
            weight = inverse_ref[c, t : t + 1, :] * available_ref[t, c].astype(jnp.float32)
            picked = pltpu.roll(picked * weight, (LANES - right) % LANES, 1)
            result.append(totals[t] + picked)
        return tuple(result)

    def one_chunk(n, count, later, totals):
        for copy in near_copies(n):
            copy.wait_recv()
        prepare(n)
        for i in range(count):
            totals = channel(n, i, totals)
            if later:
                delay_channel((n + ahead) * chunk + i)
        return totals

    totals = tuple(jnp.zeros((lag_rows, LANES), jnp.float32) for _ in range(templ_here))
    split = full_chunks - ahead
    totals = lax.fori_loop(0, split, lambda n, now: one_chunk(n, chunk, True, now), totals)
    totals = lax.fori_loop(
        split, full_chunks, lambda n, now: one_chunk(n, chunk, False, now), totals
    )
    if full_chunks < chunks:
        totals = one_chunk(full_chunks, channels - full_chunks * chunk, False, totals)

    for t in range(templ_here):
        stacks_ref[station, t] = totals[t]
    stack_copies = [
        copy_to(stacks_ref.at[station], send_stack.at[k], recv_stack.at[k], stack_peer(k))
        for k in range(1, stations)
    ]
    for copy in stack_copies:
        copy.start()
    for copy in stack_copies:
        copy.wait_recv()
    share = lag_rows // stations
    for t in range(templ_here):
        full, mine = stacks_ref[0, t], stacks_ref[0, t, pl.ds(station * share, share), :]
        for s in range(1, stations):
            full = full + stacks_ref[s, t]
            mine = mine + stacks_ref[s, t, pl.ds(station * share, share), :]
        power = jnp.sum(jnp.sum(full * full, axis=1, keepdims=True), axis=0, keepdims=True)
        mine = mine / jnp.sqrt(power / (lag_rows * LANES) + 1e-05)
        for r in range(share):
            out_ref[t : t + 1, r * LANES : (r + 1) * LANES] = mine[r : r + 1]
    for copy in stack_copies:
        copy.wait_send()
    for n in range(chunks):
        for copy in far_copies(n) + near_copies(n):
            copy.wait_send()


def shards(records, templates, offsets, available):
    channels, _ = records.shape
    templ_here, _, length = templates.shape
    blocks, stations = lax.axis_size("tmpl"), lax.axis_size("sta")
    inner = largest_divisor(blocks, 4)
    outer = blocks // inner
    lag_rows = (blocks * LANES - OFFMAX - length + 1) // LANES
    need_rows = lag_rows + (OFFMAX + LANES - 1) // LANES
    pos_rows = round_up(need_rows, 16)
    width = round_up(length + STEP - 1, LANES)
    rows = max(pos_rows + width // LANES, blocks)
    chunks = round_up(channels, CHUNK) // CHUNK
    sizes = (templ_here, channels, length, outer, inner, stations, lag_rows, need_rows, pos_rows,
             rows, width)
    macs = channels * templ_here * STEP * width * PARTS * pos_rows
    return pl.pallas_call(
        functools.partial(detect_kernel, sizes),
        out_shape=jax.ShapeDtypeStruct((templ_here, lag_rows // stations * LANES), jnp.float32),
        in_specs=[pl.BlockSpec(memory_space=pltpu.HBM)] * 4,
        out_specs=pl.BlockSpec(memory_space=pltpu.VMEM),
        scratch_shapes=[
            pltpu.SMEM(offsets.shape, jnp.int32),
            pltpu.SMEM(available.shape, jnp.int32),
            pltpu.VMEM((channels, LANES), jnp.float32),
            pltpu.VMEM((channels, templ_here, length), jnp.float32),
            pltpu.VMEM((blocks * chunks * CHUNK, LANES), jnp.float32),
            pltpu.VMEM((channels, round_up(templ_here, 8), width), jnp.float32),
            pltpu.VMEM((channels, round_up(templ_here, 8), LANES), jnp.float32),
            pltpu.VMEM((pos_rows * CHUNK, LANES), jnp.float32),
            pltpu.VMEM((PARTS * rows * CHUNK, LANES), jnp.float32),
            pltpu.VMEM((channels, templ_here * STEP, width), jnp.bfloat16),
            pltpu.VMEM((CHUNK, templ_here, pos_rows, LANES), jnp.float32),
            pltpu.VMEM((stations, templ_here, lag_rows, LANES), jnp.float32),
        ]
        + [pltpu.SemaphoreType.DMA((4,))]
        + [pltpu.SemaphoreType.DMA((inner, chunks))] * 2
        + [pltpu.SemaphoreType.DMA((outer, chunks))] * 2
        + [pltpu.SemaphoreType.DMA((stations,))] * 2,
        compiler_params=pltpu.CompilerParams(
            collective_id=0, has_side_effects=True, vmem_limit_bytes=60 * 1024 * 1024
        ),
        cost_estimate=pl.CostEstimate(
            flops=2 * macs, bytes_accessed=4 * (records.size + templates.size), transcendentals=0
        ),
    )(offsets, available, records, jnp.transpose(templates, (1, 0, 2)))


def solution(mesh):
    in_specs = (P("sta", "tmpl"), P("tmpl", "sta", None), P("tmpl", "sta"), P("tmpl", "sta"))
    out_specs = P("tmpl", "sta")
    return jax.shard_map(shards, mesh=mesh, in_specs=in_specs, out_specs=out_specs, check_vma=False)
```

```python
import functools

import jax
import jax.numpy as jnp
from jax import lax
from jax.experimental import pallas as pl
from jax.experimental.pallas import tpu as pltpu
from jax.sharding import PartitionSpec as P

OFFMAX = 425
LANES = 128
STEP = 32
PARTS = LANES // STEP


def round_up(value, unit):
    return (value + unit - 1) // unit * unit


def largest_divisor(value, most):
    return max(d for d in range(1, most + 1) if value % d == 0)


def split_three(values):
    high = values.astype(jnp.bfloat16)
    rest = values - high.astype(jnp.float32)
    middle = rest.astype(jnp.bfloat16)
    low = (rest - middle.astype(jnp.float32)).astype(jnp.bfloat16)
    return jnp.concatenate([high, middle, low], axis=1)


def detect_kernel(
    sizes, offsets_hbm, available_hbm, records_hbm, templates_hbm, out_ref,
    offsets_ref, available_ref, records_ref, templates_ref, gathered_ref, series_ref, centred_ref, inverse_ref, sums_ref, shifted_ref,
    copies_ref, picks_ref, stacks_ref, load_sem, send_near, recv_near, send_far, recv_far,
    send_stack, recv_stack,
):
    (templ_here, channels, length, outer, inner, stations, lag_rows, pos_rows, pad_rows, width,
     group, chunk) = sizes
    blocks = outer * inner
    chunks = round_up(channels, chunk) // chunk
    whole, part = length // LANES, length % LANES
    lane = lax.broadcasted_iota(jnp.int32, (1, LANES), 1)
    place, station = lax.axis_index("tmpl"), lax.axis_index("sta")
    mine_out, mine_in = place // inner, place % inner

    def far_peer(k):
        return (lax.rem(mine_out + k, outer) * inner + mine_in, station)

    def near_peer(k):
        return (mine_out * inner + lax.rem(mine_in + k, inner), station)

    def stack_peer(k):
        return (place, lax.rem(station + k, stations))

    peers = [far_peer(k) for k in range(1, outer)]
    peers += [near_peer(k) for k in range(1, inner)]
    peers += [stack_peer(k) for k in range(1, stations)]
    barrier = pltpu.get_barrier_semaphore()
    for peer in peers:
        pl.semaphore_signal(barrier, inc=1, device_id=peer, device_id_type=pl.DeviceIdType.MESH)

    loads = [
        pltpu.make_async_copy(source, target, load_sem.at[at])
        for at, (source, target) in enumerate((
            (records_hbm, records_ref), (templates_hbm, templates_ref),
            (offsets_hbm, offsets_ref), (available_hbm, available_ref),
        ))
    ]
    for load in loads:
        load.start()

    def own_rows(n):
        first = ((n * inner + mine_in) * outer + mine_out) * chunk
        return gathered_ref.at[pl.ds(pl.multiple_of(first, 8), chunk)]

    def line_rows(n):
        first = (n * inner + mine_in) * outer * chunk
        return gathered_ref.at[pl.ds(pl.multiple_of(first, 8), outer * chunk)]

    loads[0].wait()
    for n in range(chunks):
        rows = records_ref[n * chunk : min((n + 1) * chunk, channels), :]
        if rows.shape[0] < chunk:
            tail = jnp.zeros((chunk - rows.shape[0], LANES), jnp.float32)
            rows = jnp.concatenate([rows, tail], axis=0)
        own_rows(n)[...] = rows
    pl.semaphore_wait(barrier, len(peers))

    def copy_to(part_ref, send_sem, recv_sem, peer):
        return pltpu.make_async_remote_copy(
            src_ref=part_ref, dst_ref=part_ref, send_sem=send_sem, recv_sem=recv_sem,
            device_id=peer, device_id_type=pl.DeviceIdType.MESH,
        )

    def far_copies(n):
        return [
            copy_to(own_rows(n), send_far.at[k, n], recv_far.at[k, n], far_peer(k))
            for k in range(1, outer)
        ]

    def near_copies(n):
        return [
            copy_to(line_rows(n), send_near.at[k, n], recv_near.at[k, n], near_peer(k))
            for k in range(1, inner)
        ]

    for n in range(chunks):
        for copy in far_copies(n):
            copy.start()

    series_ref[...] = jnp.zeros_like(series_ref)
    sums_ref[...] = jnp.zeros_like(sums_ref)
    centred_ref[...] = jnp.zeros_like(centred_ref)
    for load in loads[1:]:
        load.wait()

    def delay_group(g, carry):
        for i in range(group):
            c = g * group + i
            shapes = templates_ref[c]
            centred = shapes - jnp.sum(shapes, axis=1, keepdims=True) / length
            power = jnp.sum(centred * centred, axis=1, keepdims=True)
            centred_ref[i, :templ_here, :length] = centred
            inverse_ref[c, :templ_here, :] = jnp.broadcast_to(
                1.0 / jnp.sqrt(power + 1e-05), (templ_here, LANES)
            )
            for t in range(templ_here):
                wave = jnp.broadcast_to(centred_ref[i, t : t + 1, :], (8, width))
                first = pltpu.roll(wave, 0, 1, stride=1, stride_axis=0)
                for h in range(STEP // 16):
                    pair = [
                        first if s == 0 else pltpu.roll(first, s, 1)
                        for s in (16 * h, 16 * h + 8)
                    ]
                    copies_ref[c, t * STEP + 16 * h : t * STEP + 16 * h + 16, :] = (
                        jnp.concatenate(pair, axis=0).astype(jnp.bfloat16)
                    )
        return carry

    groups = channels // group
    full_chunks = channels // chunk
    inline = full_chunks // 2
    ahead = groups - inline * (chunk // group)
    each = ahead // chunks

    def forward(n, carry):
        lax.fori_loop(n * each, n * each + each, delay_group, 0)
        for copy in far_copies(n):
            copy.wait_recv()
        for copy in near_copies(n):
            copy.start()
        return carry

    lax.fori_loop(0, chunks, forward, 0)
    lax.fori_loop(chunks * each, ahead, delay_group, 0)

    row = lax.broadcasted_iota(jnp.int32, (LANES, 2 * LANES), 0)
    column = lax.broadcasted_iota(jnp.int32, (LANES, 2 * LANES), 1)
    ones = jnp.where((row < column) | (column >= LANES), 1.0, 0.0).astype(jnp.bfloat16)
    ones = jnp.concatenate([ones, ones, ones], axis=0)

    def block_sums(n, count):
        for i in range(count):
            c = n * chunk + i
            for o in range(outer):
                series_ref[c, o * inner : (o + 1) * inner, :] = gathered_ref[
                    pl.ds(n * blocks * chunk + o * chunk + i, inner, stride=outer * chunk), :
                ]
        block = jnp.concatenate(
            [series_ref[n * chunk + i, :blocks, :] for i in range(count)], axis=0
        )
        for kind in range(2):
            parts = split_three(block if kind == 0 else block * block)
            sums = jnp.dot(parts, ones, preferred_element_type=jnp.float32)
            for i in range(count):
                sums_ref[i, kind, :blocks, :] = sums[i * blocks : (i + 1) * blocks]

    def scale_of(i):
        windows = []
        for kind in range(2):
            inside = lambda first: sums_ref[i, kind, first : first + pos_rows, :LANES]
            total = lambda first: sums_ref[i, kind, first : first + pos_rows, LANES:]
            near, far = inside(whole), inside(whole + 1)
            if part:
                near = pltpu.roll(near, LANES - part, 1)
                far = pltpu.roll(far, LANES - part, 1)
            window = jnp.where(lane < LANES - part, near, far + total(whole)) - inside(0)
            for b in range(whole):
                window = window + total(b)
            windows.append(window)
        energy = windows[1] - windows[0] * windows[0] / length
        return lax.rsqrt(energy + 1e-05)

    def channel(c, inside_chunk, slot, totals):
        reach = pad_rows - 8
        for u in range(1, PARTS):
            shifted_ref[slot, u, :reach, :] = pltpu.roll(
                series_ref[c, :reach, :], LANES - STEP * u, 1
            )

        def frame(u, j):
            if u == 0:
                return series_ref[c, j : j + pos_rows, :].astype(jnp.bfloat16)
            return jnp.where(
                lane < LANES - STEP * u,
                shifted_ref[slot, u, j : j + pos_rows, :],
                shifted_ref[slot, u, j + 1 : j + 1 + pos_rows, :],
            ).astype(jnp.bfloat16)

        frames = jnp.concatenate(
            [
                jnp.concatenate(
                    [frame(u, j) for j in range(width // LANES)],
                    axis=1,
                )
                for u in range(PARTS)
            ],
            axis=0,
        )
        product = lax.dot_general(
            frames, copies_ref[c], (((1,), (1,)), ((), ())), preferred_element_type=jnp.float32
        )
        scale = scale_of(inside_chunk)
        turned = {}
        for u in range(PARTS):
            piece = product[u * pos_rows : (u + 1) * pos_rows]
            for k in range(PARTS):
                turned[u, k] = piece if k == 0 else pltpu.roll(piece, STEP * k, 1)
        result = []
        for t in range(templ_here):
            values = turned[0, (-t) % PARTS]
            for u in range(1, PARTS):
                values = jnp.where(lane >= STEP * u, turned[u, (u - t) % PARTS], values)
            picks_ref[slot, t] = values * scale
            offset = offsets_ref[t, c]
            down, right = offset // LANES, offset % LANES
            wanted = jnp.where(lane < right, down + 1, down)
            picked = picks_ref[slot, t, :lag_rows, :]
            for d in range(1, (OFFMAX + LANES - 1) // LANES + 1):
                picked = jnp.where(wanted == d, picks_ref[slot, t, d : d + lag_rows, :], picked)
            weight = inverse_ref[c, t : t + 1, :] * available_ref[t, c].astype(jnp.float32)
            picked = pltpu.roll(picked * weight, (LANES - right) % LANES, 1)
            result.append(totals[t] + picked)
        return tuple(result)

    def one_chunk(n, count, later, totals):
        for copy in near_copies(n):
            copy.wait_recv()
        block_sums(n, count)

        def channel_group(g, totals):
            for i in range(group):
                totals = channel(n * chunk + g * group + i, g * group + i, i, totals)
            if later:
                delay_group(ahead + n * (chunk // group) + g, 0)
            return totals

        return lax.fori_loop(0, count // group, channel_group, totals)

    totals = tuple(jnp.zeros((lag_rows, LANES), jnp.float32) for _ in range(templ_here))
    totals = lax.fori_loop(0, inline, lambda n, now: one_chunk(n, chunk, True, now), totals)
    totals = lax.fori_loop(
        inline, full_chunks, lambda n, now: one_chunk(n, chunk, False, now), totals
    )
    if full_chunks < chunks:
        totals = one_chunk(full_chunks, channels - full_chunks * chunk, False, totals)

    for t in range(templ_here):
        stacks_ref[station, t] = totals[t]
    stack_copies = [
        copy_to(stacks_ref.at[station], send_stack.at[k], recv_stack.at[k], stack_peer(k))
        for k in range(1, stations)
    ]
    for copy in stack_copies:
        copy.start()
    for copy in stack_copies:
        copy.wait_recv()
    share = lag_rows // stations
    for t in range(templ_here):
        full, mine = stacks_ref[0, t], stacks_ref[0, t, pl.ds(station * share, share), :]
        for s in range(1, stations):
            full = full + stacks_ref[s, t]
            mine = mine + stacks_ref[s, t, pl.ds(station * share, share), :]
        power = jnp.sum(jnp.sum(full * full, axis=1, keepdims=True), axis=0, keepdims=True)
        mine = mine / jnp.sqrt(power / (lag_rows * LANES) + 1e-05)
        for r in range(share):
            out_ref[t : t + 1, r * LANES : (r + 1) * LANES] = mine[r : r + 1]
    for copy in stack_copies:
        copy.wait_send()
    for n in range(chunks):
        for copy in far_copies(n) + near_copies(n):
            copy.wait_send()


def shards(records, templates, offsets, available):
    channels, _ = records.shape
    templ_here, _, length = templates.shape
    blocks, stations = lax.axis_size("tmpl"), lax.axis_size("sta")
    inner = largest_divisor(blocks, 4)
    outer = blocks // inner
    lag_rows = (blocks * LANES - OFFMAX - length + 1) // LANES
    reach_rows = (OFFMAX + LANES - 1) // LANES
    pos_rows = round_up(lag_rows + reach_rows, 16)
    width = round_up(length + STEP - 1, LANES)
    pad_rows = round_up(max(pos_rows + width // LANES, blocks) + 1, 8) + 8
    group = largest_divisor(channels, 4)
    slot_rows = round_up(channels, 8)
    chunk = 16 if slot_rows % 16 == 0 else 8
    chunks = slot_rows // chunk
    sizes = (templ_here, channels, length, outer, inner, stations, lag_rows, pos_rows, pad_rows,
             width, group, chunk)
    macs = channels * templ_here * STEP * width * PARTS * pos_rows
    return pl.pallas_call(
        functools.partial(detect_kernel, sizes),
        out_shape=jax.ShapeDtypeStruct((templ_here, lag_rows // stations * LANES), jnp.float32),
        in_specs=[pl.BlockSpec(memory_space=pltpu.HBM)] * 4,
        out_specs=pl.BlockSpec(memory_space=pltpu.VMEM),
        scratch_shapes=[
            pltpu.SMEM(offsets.shape, jnp.int32),
            pltpu.SMEM(available.shape, jnp.int32),
            pltpu.VMEM((channels, LANES), jnp.float32),
            pltpu.VMEM((channels, templ_here, length), jnp.float32),
            pltpu.VMEM((blocks * slot_rows, LANES), jnp.float32),
            pltpu.VMEM((channels, pad_rows, LANES), jnp.float32),
            pltpu.VMEM((group, round_up(templ_here, 8), width), jnp.float32),
            pltpu.VMEM((channels, round_up(templ_here, 8), LANES), jnp.float32),
            pltpu.VMEM((chunk, 2, pad_rows, 2 * LANES), jnp.float32),
            pltpu.VMEM((group, PARTS, pad_rows, LANES), jnp.float32),
            pltpu.VMEM((channels, templ_here * STEP, width), jnp.bfloat16),
            pltpu.VMEM((group, templ_here, pos_rows, LANES), jnp.float32),
            pltpu.VMEM((stations, templ_here, lag_rows, LANES), jnp.float32),
        ]
        + [pltpu.SemaphoreType.DMA((4,))]
        + [pltpu.SemaphoreType.DMA((inner, chunks))] * 2
        + [pltpu.SemaphoreType.DMA((outer, chunks))] * 2
        + [pltpu.SemaphoreType.DMA((stations,))] * 2,
        compiler_params=pltpu.CompilerParams(
            collective_id=0, has_side_effects=True, vmem_limit_bytes=60 * 1024 * 1024
        ),
        cost_estimate=pl.CostEstimate(
            flops=2 * macs, bytes_accessed=4 * (records.size + templates.size), transcendentals=0
        ),
    )(offsets, available, records, jnp.transpose(templates, (1, 0, 2)))


def solution(mesh):
    in_specs = (P("sta", "tmpl"), P("tmpl", "sta", None), P("tmpl", "sta"), P("tmpl", "sta"))
    out_specs = P("tmpl", "sta")
    return jax.shard_map(shards, mesh=mesh, in_specs=in_specs, out_specs=out_specs, check_vma=False)
```
